32 devices in a mesh: section: 8 (over y, x, core), tensor: 4 (over z).
Axes of the slice: x: 2, y: 2, z: 4, core: 2. Of those that a mesh axis runs over, the one named last changes fastest.
Arguments:
- fwd_input: bfloat16 [8, 64, 4608], P('section', None, 'tensor'), may hold values from -6 to 6
- bwd_grad: bfloat16 [8, 64, 4608], P('section', None, 'tensor'), may hold values from -6 to 6
- parked: bfloat16 [8, 64, 4608], P('section', None, 'tensor'), may hold values from -6 to 6
- norm_gain: float32 [8, 4608], P('section'), may hold values from 0.25 to 1.75
- w_query: bfloat16 [8, 4608, 512], P('section', None, 'tensor'), may hold values from -1 to 1
- w_key: bfloat16 [8, 4608, 512], P('section', None, 'tensor'), may hold values from -1 to 1
- w_value: bfloat16 [8, 4608, 512], P('section', None, 'tensor'), may hold values from -0.09375 to 0.09375
- w_out: bfloat16 [8, 512, 4608], P('section', 'tensor'), may hold values from -0.25 to 0.25
- offsets: int32 [8, 2, 8], P('section'), may hold values from 0 to 56, as said below
- mirror: int32 [8], replicated, may hold values from 0 to 7, as said below
Outputs:
- next_input: bfloat16 [8, 64, 4608], P('section', None, 'tensor')
- prev_grad: bfloat16 [8, 64, 4608], P('section', None, 'tensor')
- parked_new: bfloat16 [8, 64, 4608], P('section', None, 'tensor')
The draws below stay inside these ranges and needn't reach their ends.
Inputs may be any that keep to these rules, and one draw needn't show every extreme that they name: Each row offsets[s, j] holds the numbers 0, 8, ..., 56 once each. mirror[t] = t XOR m for one m with 8 / 2 <= m < 8, so sections of the first half pair with sections of the second half.
All inputs are finite; a program needn't handle non-finite values.
Results may differ from the reference program's by a relative error of at most 0.018.
Values may be sent and summed in bfloat16 or wider, within the bound.
A program may use at most 64 MiB of HBM per device.

```python
import math
import jax
import jax.numpy as jnp
from jax import lax

DW = 4608
HD = 64
HEADS_DEV = 2
HEADS = 8
SPAN = 8
NCH = 8
ROWS = 64
N_SECTION = 8
N_TENSOR = 4


def projection_draw(key, salt):
    scale = DW ** (-0.5)
    salted = jax.random.fold_in(key, salt)

    def one_section(section):
        noise = jax.random.truncated_normal(jax.random.fold_in(salted, section), -6.0, 6.0, (DW, HEADS * HD), jnp.float32) * scale
        return noise
    return lax.map(one_section, jnp.arange(N_SECTION, dtype=jnp.int32)).astype(jnp.bfloat16)


def activation_draw(key, salt):
    salted = jax.random.fold_in(key, salt)

    def one_section(section):
        section_key = jax.random.fold_in(salted, section)
        rows = jax.random.truncated_normal(section_key, -6.0, 6.0, (ROWS, DW), jnp.float32)
        return jnp.clip(rows, -6.0, 6.0)
    return lax.map(one_section, jnp.arange(N_SECTION, dtype=jnp.int32)).astype(jnp.bfloat16)


def draw_w_query(key, part):
    return projection_draw(key, 31)


def draw_w_key(key, part):
    return projection_draw(key, 37)


def draw_fwd_input(key, part):
    return activation_draw(key, 41)


def draw_parked(key, part):
    return activation_draw(key, 43)


def draw_offsets(key, part):
    row_keys = jax.random.split(jax.random.fold_in(key, 11), N_SECTION * 2)
    orders = jax.vmap(lambda row_key: jax.random.permutation(row_key, NCH))(row_keys)
    return (orders.reshape(N_SECTION, 2, NCH) * SPAN).astype(jnp.int32)


def draw_mirror(key, part):
    xor_mask = jax.random.randint(jax.random.fold_in(key, 23), (), N_SECTION // 2, N_SECTION)
    return jnp.bitwise_xor(jnp.arange(N_SECTION, dtype=jnp.int32), xor_mask.astype(jnp.int32)).astype(jnp.int32)


def block_scale(key, dims, pieces, least, largest):
    gain, own = 1.0, jax.random.fold_in(key, 6)
    for axis_at, parts in pieces:
        heights = jnp.exp(jax.random.uniform(jax.random.fold_in(own, axis_at), (parts,), jnp.float32, least / len(pieces), largest / len(pieces)))
        gain = gain * jnp.repeat(heights, dims[axis_at] // parts).reshape([-1 if axis == axis_at else 1 for axis in range(len(dims))])
    return gain


def normal_values(own_key, shape, width, most, shards=(), held_as=jnp.bfloat16):
    result = jax.random.normal(own_key, shape, jnp.float32) * width
    if len(shards) > 0:
        result = block_scale(own_key, shape, shards, -0.22, 0.18) * result
    return jnp.clip(result, min=-most, max=most).astype(held_as)


def setup_inputs(seed: int = 0) -> dict:
    key_of = jax.random.split(jax.random.key(seed), 11)
    return {
        "fwd_input": draw_fwd_input(jax.random.fold_in(key_of[10], 71), 0),
        "bwd_grad": normal_values(key_of[1], (N_SECTION, ROWS, DW), 1.0, 6.0, ((0, 8), (2, 4))),
        "parked": draw_parked(jax.random.fold_in(key_of[10], 71), 0),
        "norm_gain": jnp.clip(1.0 + 0.15 * jax.random.normal(key_of[3], (N_SECTION, DW), jnp.float32), 0.25, 1.75),
        "w_query": draw_w_query(jax.random.fold_in(key_of[10], 71), 0),
        "w_key": draw_w_key(jax.random.fold_in(key_of[10], 71), 0),
        "w_value": normal_values(key_of[6], (N_SECTION, DW, HEADS * HD), DW ** -0.5, 0.09375, ((0, 8), (2, 4))),
        "w_out": normal_values(key_of[7], (N_SECTION, HEADS * HD, DW), (HEADS * HD) ** -0.5, 0.25, ((0, 8), (1, 4))),
        "offsets": draw_offsets(jax.random.fold_in(key_of[10], 71), 0),
        "mirror": draw_mirror(jax.random.fold_in(key_of[10], 71), 0),
    }


def token_positions(starts, row_count):
    rows_iota = jnp.arange(row_count, dtype=jnp.int32)
    block_id = rows_iota // SPAN
    chosen = block_id[:, None] == jnp.arange(starts.shape[0], dtype=jnp.int32)[None, :]
    return lax.optimization_barrier(jnp.sum(jnp.where(chosen, starts[None, :], 0), axis=1)).astype(jnp.int32) + rows_iota % SPAN

def branch(inputs, norm_scale, query_part, key_part, value_part, out_part, places):
    row_count = inputs.shape[0]
    head_count = query_part.shape[1] // HD
    widened = inputs.astype(jnp.float32)
    inverse = lax.rsqrt(lax.optimization_barrier(jnp.mean(widened * widened, axis=1, keepdims=True)) + 1e-05)
    normed = (widened * inverse * norm_scale[None, :]).astype(jnp.bfloat16)
    queries = jnp.dot(normed, query_part, preferred_element_type=jnp.float32).astype(jnp.bfloat16).reshape(row_count, head_count, HD)
    key_rows = jnp.dot(normed, key_part, preferred_element_type=jnp.float32).astype(jnp.bfloat16).reshape(row_count, head_count, HD)
    value_rows = jnp.dot(normed, value_part, preferred_element_type=jnp.float32).astype(jnp.bfloat16).reshape(row_count, head_count, HD)
    scores = jnp.einsum('qhd,khd->hqk', queries.astype(jnp.float32), key_rows.astype(jnp.float32)) / math.sqrt(HD)
    allowed = places[None, :, None] >= places[None, None, :]
    scores = jnp.where(allowed, scores, -1e+30)
    row_max = lax.optimization_barrier(jnp.max(scores, axis=2, keepdims=True))
    exp_scores = jnp.exp(scores - row_max)
    weights = (exp_scores / lax.optimization_barrier(jnp.sum(exp_scores, axis=2, keepdims=True))).astype(jnp.bfloat16)
    context = jnp.einsum('hqk,khd->qhd', weights.astype(jnp.float32), value_rows.astype(jnp.float32)).astype(jnp.bfloat16)
    return jnp.dot(context.reshape(row_count, head_count * HD), out_part, preferred_element_type=jnp.float32)

def rounded(term):
    return lax.optimization_barrier(term.astype(jnp.bfloat16)).astype(jnp.float32)

def reference(fwd_input, bwd_grad, parked, norm_gain, w_query, w_key, w_value, w_out, offsets, mirror):
    group_width = HEADS_DEV * HD
    fetched = jnp.take(parked, mirror, axis=0)

    def one_section(section_index):
        fwd_rows = fwd_input[section_index]
        grad_rows = bwd_grad[section_index]
        stashed = fetched[section_index]
        scale_row = norm_gain[section_index]
        pos_fwd = token_positions(offsets[section_index, 0], ROWS)
        pos_bwd = token_positions(offsets[section_index, 1], ROWS)

        def one_group(group):
            first_col = (group * group_width).astype(jnp.int32)
            query_part = lax.dynamic_slice_in_dim(w_query[section_index], first_col, group_width, 1)
            key_part = lax.dynamic_slice_in_dim(w_key[section_index], first_col, group_width, 1)
            value_part = lax.dynamic_slice_in_dim(w_value[section_index], first_col, group_width, 1)
            out_part = lax.dynamic_slice_in_dim(w_out[section_index], first_col, group_width, 0)
            forward_term = branch(fwd_rows, scale_row, query_part, key_part, value_part, out_part, pos_fwd)

            def stashed_branch(layer_in):
                return branch(layer_in, scale_row, query_part, key_part, value_part, out_part, pos_bwd)
            unused, pullback = jax.vjp(stashed_branch, stashed)
            back_term, = pullback(grad_rows.astype(jnp.float32))
            return (rounded(forward_term), rounded(back_term.astype(jnp.float32)))
        forward_parts, back_parts = lax.map(one_group, jnp.arange(N_TENSOR, dtype=jnp.int32))
        layer_out = (fwd_rows.astype(jnp.float32) + lax.optimization_barrier(jnp.sum(forward_parts, axis=0))).astype(jnp.bfloat16)
        grad_out = (grad_rows.astype(jnp.float32) + lax.optimization_barrier(jnp.sum(back_parts, axis=0))).astype(jnp.bfloat16)
        return (layer_out, grad_out)
    layer_outs, grad_outs = lax.map(one_section, jnp.arange(N_SECTION, dtype=jnp.int32))
    zero_block = jnp.zeros_like(layer_outs[:1])
    next_input = jnp.concatenate([zero_block, layer_outs[:-1]], axis=0)
    prev_grad = jnp.concatenate([grad_outs[1:], zero_block], axis=0)
    parked_new = jnp.take(fwd_input, mirror, axis=0)
    return (next_input, prev_grad, parked_new)
```

```python
import functools

import jax
import jax.numpy as jnp
from jax import lax
from jax.experimental import pallas as pl
from jax.experimental.pallas import tpu as pltpu
from jax.sharding import PartitionSpec as P

HD = 64
SPAN = 8
MESH = pl.DeviceIdType.MESH
F32 = jnp.float32
BF16 = jnp.bfloat16

NN = (((1,), (0,)), ((), ()))
NT = (((1,), (1,)), ((), ()))
TN = (((0,), (0,)), ((), ()))


def dot(a, b, dims):
    return lax.dot_general(a, b, dims, preferred_element_type=F32)


def within(value, size):
    return jnp.logical_and(value >= 0, value < size)


def kernel(
    n_tensor, n_section, n_bits, blocked,
    fwd_ref, grad_ref, park_ref, gain_ref, wq_ref, wk_ref, wv_ref, wo_hbm, offs_ref, mirror_ref,
    next_ref, prev_ref, pnew_ref,
    w, wo, full, part, arrived, acc, stage, zeros, qkv, ssq, dctx, dqkv, got, cur,
    ag_send, ag_recv, rs_send, rs_recv, swap_send, swap_recv, pass_send, pass_recv, local,
):
    t = lax.axis_index("tensor")
    s = lax.axis_index("section")
    rows, width = fwd_ref.shape[1], fwd_ref.shape[2]
    features = width * n_tensor
    cols = wq_ref.shape[2]
    heads = cols // HD
    blocks = offs_ref.shape[2]

    def mate(bit):
        return s + (1 - 2 * ((s // (1 << bit)) % 2)) * (1 << bit)

    barrier = pltpu.get_barrier_semaphore()

    def greet(ok, where):
        @pl.when(ok)
        def _():
            pl.semaphore_signal(barrier, inc=1, device_id=where, device_id_type=MESH)

    greet(t > 0, {"tensor": t - 1})
    greet(t < n_tensor - 1, {"tensor": t + 1})
    greet(s > 0, {"section": s - 1})
    greet(s < n_section - 1, {"section": s + 1})
    for bit in range(n_bits):
        pl.semaphore_signal(barrier, inc=1, device_id={"section": mate(bit)}, device_id_type=MESH)

    loads = [
        pltpu.make_async_copy(fwd_ref.at[0], full.at[0, t], local.at[0]),
        pltpu.make_async_copy(grad_ref.at[0], full.at[1, t], local.at[1]),
        pltpu.make_async_copy(wq_ref.at[0], w.at[:, pl.ds(0, cols)], local.at[2]),
        pltpu.make_async_copy(wk_ref.at[0], w.at[:, pl.ds(cols, cols)], local.at[3]),
        pltpu.make_async_copy(wv_ref.at[0], w.at[:, pl.ds(2 * cols, cols)], local.at[4]),
        pltpu.make_async_copy(wo_hbm if blocked else wo_hbm.at[0], wo, local.at[5]),
    ]
    for load in loads:
        load.start()

    def one(ok):
        return jnp.where(ok, 1, 0)

    pl.semaphore_wait(
        barrier,
        n_bits + one(t > 0) + one(t < n_tensor - 1) + one(s > 0) + one(s < n_section - 1),
    )

    def ag_copy(a, b, way, src):
        return pltpu.make_async_remote_copy(
            src_ref=src, dst_ref=full.at[a, b],
            send_sem=ag_send.at[a, way, b], recv_sem=ag_recv.at[a, b],
            device_id={"tensor": t + 1 - 2 * way}, device_id_type=MESH,
        )

    def ag_own(a, src):
        for way in range(2):
            @pl.when(within(t + 1 - 2 * way, n_tensor))
            def _():
                ag_copy(a, t, way, src).start()

    def ag_round(a, k, consume):
        def step(way, carry):
            b = t + (1 + k) * (2 * way - 1)

            @pl.when(within(b, n_tensor))
            def _():
                ag_copy(a, b, way, full.at[a, b]).wait_recv()

                @pl.when(within(t + 1 - 2 * way, n_tensor))
                def _():
                    ag_copy(a, b, way, full.at[a, b]).start()

                consume(b)

            return carry

        lax.fori_loop(0, 2, step, 0)

    def swap_copy(a, bit):
        if bit == n_bits - 1:
            src = (park_ref if a == 0 else fwd_ref).at[0]
        else:
            src = got.at[a, bit + 1] if bit == n_bits - 2 else cur.at[a, bit + 1]
        return pltpu.make_async_remote_copy(
            src_ref=src, dst_ref=got.at[a, bit],
            send_sem=swap_send.at[a, bit], recv_sem=swap_recv.at[a, bit],
            device_id={"section": mate(bit)}, device_id_type=MESH,
        )

    def swap_finish(a, bit):
        swap_copy(a, bit).wait_recv()
        if bit < n_bits - 1:
            mine = got[a, bit + 1] if bit == n_bits - 2 else cur[a, bit + 1]
            flag = lax.shift_right_logical(mirror_ref[0], bit) & 1
            chosen = jnp.full((rows, width), flag, jnp.int32) == 1
            cur[a, bit] = jnp.where(chosen, got[a, bit].astype(F32), mine.astype(F32)).astype(BF16)
        if bit > 0:
            swap_copy(a, bit - 1).start()

    swap_copy(0, n_bits - 1).start()
    ag_own(0, fwd_ref.at[0])
    ag_own(1, grad_ref.at[0])

    def gain_block(b):
        if blocked:
            return gain_ref[b]
        return gain_ref[0:1, pl.ds(pl.multiple_of(b * width, 128), width)]

    def w_rows(b):
        return w[pl.ds(pl.multiple_of(b * width, 64), width), :]

    def wo_block(b):
        if blocked:
            return wo[b]
        return wo[:, pl.ds(pl.multiple_of(b * width, 128), width)]

    def add_qkv(a, b):
        x = full[a, b].astype(F32)
        ssq[...] += jnp.broadcast_to(jnp.sum(x * x, axis=1, keepdims=True), ssq.shape)
        qkv[...] += dot((x * gain_block(b)).astype(BF16), w_rows(b), NN)

    def add_dctx(b):
        dctx[...] += dot(full[1, b], wo_block(b), NT)

    def clear():
        ssq[...] = jnp.zeros_like(ssq)
        qkv[...] = jnp.zeros_like(qkv)

    clear()
    dctx[...] = jnp.zeros_like(dctx)
    zeros[...] = jnp.zeros_like(zeros)
    for load in loads:
        load.wait()
    add_qkv(0, t)
    add_dctx(t)

    first = [functools.partial(swap_finish, 0, bit) for bit in reversed(range(n_bits))]
    first[0]()

    def round_one(k, carry):
        ag_round(0, k, functools.partial(add_qkv, 0))
        ag_round(1, k, add_dctx)

        @pl.when(k == 0)
        def _():
            for finish in first[1:]:
                finish()
            full[2, t] = cur[0, 0]
            ag_own(2, full.at[2, t])
            swap_copy(1, n_bits - 1).start()

        return carry

    lax.fori_loop(0, n_tensor - 1, round_one, 0)

    lane = lax.broadcasted_iota(jnp.int32, (rows, cols), 1)

    def masked(value):
        return jnp.concatenate(
            [jnp.where(lane // HD == h, value, 0.0) for h in range(heads)], axis=0
        ).astype(BF16)

    def merged(stacked):
        total = stacked[:rows]
        for h in range(1, heads):
            total = jnp.where(lane // HD == h, stacked[h * rows:(h + 1) * rows], total)
        return total

    def places(which, axis):
        index = lax.broadcasted_iota(jnp.int32, (heads * rows, rows), axis) & (rows - 1)
        block = lax.shift_right_logical(index, 3)
        value = index & (SPAN - 1)
        for b in range(blocks):
            value = value + jnp.where(block == b, offs_ref[0, which, b], 0)
        return value

    def attend(which):
        inverse = lax.rsqrt(ssq[:, 0:1] / features + 1e-05)
        scaled = qkv[...] * inverse
        q = masked(scaled[:, :cols])
        k = scaled[:, cols:2 * cols].astype(BF16)
        v = scaled[:, 2 * cols:].astype(BF16)
        scores = dot(q, k, NT) * (HD ** -0.5)
        scores = jnp.where(places(which, 0) >= places(which, 1), scores, -1e30)
        expd = jnp.exp(scores - jnp.max(scores, axis=1, keepdims=True))
        weights = expd / jnp.sum(expd, axis=1, keepdims=True)
        return inverse, q, k, v, weights

    def rs_copy(a, d, way):
        return pltpu.make_async_remote_copy(
            src_ref=part.at[a, d], dst_ref=arrived.at[a, way, d],
            send_sem=rs_send.at[a, d], recv_sem=rs_recv.at[a, way, d],
            device_id={"tensor": t + 1 - 2 * way}, device_id_type=MESH,
        )

    def rs_begin(a, term):
        def step(i, carry):
            d = jnp.where(t < n_tensor // 2, n_tensor - 1 - i, i)
            part[a, d] = term(d).astype(BF16)

            @pl.when(jnp.logical_and(t == 0, d > 0))
            def _():
                rs_copy(a, d, 0).start()

            @pl.when(jnp.logical_and(t == n_tensor - 1, d < n_tensor - 1))
            def _():
                rs_copy(a, d, 1).start()

            return carry

        lax.fori_loop(0, n_tensor, step, 0)
        acc[...] = full[a, t].astype(F32) + part[a, t].astype(F32)

    def rs_round(a, j):
        def step(way, carry):
            d = (1 - way) * (n_tensor - 1 - j) + way * j
            sign = 1 - 2 * way
            ahead = (d - t) * sign

            @pl.when(jnp.logical_and(ahead >= 0, within(t - sign, n_tensor)))
            def _():
                rs_copy(a, d, way).wait_recv()

                @pl.when(ahead > 0)
                def _():
                    part[a, d] = (part[a, d].astype(F32) + arrived[a, way, d].astype(F32)).astype(BF16)
                    rs_copy(a, d, way).start()

                @pl.when(ahead == 0)
                def _():
                    acc[...] += arrived[a, way, d].astype(F32)

            return carry

        lax.fori_loop(0, 2, step, 0)

    def pass_copy(a):
        return pltpu.make_async_remote_copy(
            src_ref=stage.at[a], dst_ref=(next_ref if a == 0 else prev_ref).at[0],
            send_sem=pass_send.at[a], recv_sem=pass_recv.at[a],
            device_id={"section": s + 1 - 2 * a}, device_id_type=MESH,
        )

    def pass_on(a):
        stage[a] = acc[...].astype(BF16)

        @pl.when(within(s + 1 - 2 * a, n_section))
        def _():
            pass_copy(a).start()

    def zero_copy(a):
        return pltpu.make_async_copy(zeros, (next_ref if a == 0 else prev_ref).at[0], local.at[6])

    @pl.when(s == 0)
    def _():
        zero_copy(0).start()

    @pl.when(s == n_section - 1)
    def _():
        zero_copy(1).start()

    inverse, q, k, v, weights = attend(0)
    context = merged(dot(weights.astype(BF16), v, NN)).astype(BF16)
    rs_begin(0, lambda d: dot(context, wo_block(d), NN))
    clear()
    add_qkv(2, t)

    second = [functools.partial(swap_finish, 1, bit) for bit in reversed(range(n_bits))]

    def round_two(k, carry):
        ag_round(2, k, functools.partial(add_qkv, 2))
        rs_round(0, k)

        @pl.when(k == 0)
        def _():
            for finish in second:
                finish()
            pltpu.make_async_copy(cur.at[1, 0], pnew_ref.at[0], local.at[7]).start()

        return carry

    lax.fori_loop(0, n_tensor - 1, round_two, 0)
    pass_on(0)

    inverse, q, k, v, weights = attend(1)
    dc = masked(dctx[...])
    dweights = dot(dc, v, NT)
    dscores = weights * (dweights - jnp.sum(dweights * weights, axis=1, keepdims=True))
    dscores = (dscores * (HD ** -0.5)).astype(BF16)
    dqkv[:, :cols] = merged(dot(dscores, k, NN)).astype(BF16)
    dqkv[:, cols:2 * cols] = dot(dscores, q, TN).astype(BF16)
    dqkv[:, 2 * cols:] = dot(weights.astype(BF16), dc, TN).astype(BF16)
    pull = dqkv[...]
    along = jnp.sum(pull.astype(F32) * qkv[...], axis=1, keepdims=True)
    along = along * inverse * inverse * inverse / features

    def back_term(d):
        dnormed = dot(pull, w_rows(d), NT)
        return inverse * (dnormed * gain_block(d)) - full[2, d].astype(F32) * along

    rs_begin(1, back_term)

    def round_three(j, carry):
        rs_round(1, j)
        return carry

    lax.fori_loop(0, n_tensor - 1, round_three, 0)
    pass_on(1)

    def drain(b, carry):
        for way in range(2):
            sent = (b <= t) if way == 0 else (b >= t)

            @pl.when(jnp.logical_and(sent, within(t + 1 - 2 * way, n_tensor)))
            def _():
                for a in range(3):
                    ag_copy(a, b, way, full.at[a, b]).wait_send()

        @pl.when(b != t)
        def _():
            for a in range(2):
                rs_copy(a, b, 0).wait_send()

        return carry

    lax.fori_loop(0, n_tensor, drain, 0)
    for a in range(2):
        for bit in range(n_bits):
            swap_copy(a, bit).wait_send()
    pltpu.make_async_copy(cur.at[1, 0], pnew_ref.at[0], local.at[7]).wait()
    for a in range(2):
        edge = 0 if a == 0 else n_section - 1

        @pl.when(s == edge)
        def _():
            zero_copy(a).wait()

        @pl.when(s != edge)
        def _():
            pass_copy(a).wait_recv()

        @pl.when(within(s + 1 - 2 * a, n_section))
        def _():
            pass_copy(a).wait_send()


def local_step(n_tensor, n_section, fwd, grad, park, gain, wq, wk, wv, wo, offs, mirror):
    _, rows, width = fwd.shape
    features = gain.shape[1]
    cols = wq.shape[2]
    n_bits = n_section.bit_length() - 1
    blocked = width % 128 != 0
    if blocked:
        gain = gain.reshape(n_tensor, 1, width)
        wo = wo[0].reshape(cols, n_tensor, width).transpose(1, 0, 2)
    heads = cols // HD
    any_spec = pl.BlockSpec(memory_space=pl.ANY)
    vmem = pl.BlockSpec(memory_space=pltpu.VMEM)
    smem = pl.BlockSpec(memory_space=pltpu.SMEM)
    out = jax.ShapeDtypeStruct(fwd.shape, BF16)
    dma = pltpu.SemaphoreType.DMA
    return pl.pallas_call(
        functools.partial(kernel, n_tensor, n_section, n_bits, blocked),
        out_shape=(out, out, out),
        in_specs=[any_spec] * 3 + [vmem] + [any_spec] * 4 + [smem] * 2,
        out_specs=(any_spec,) * 3,
        scratch_shapes=[
            pltpu.VMEM((features, 3 * cols), BF16),
            pltpu.VMEM((n_tensor, cols, width) if blocked else (cols, features), BF16),
            pltpu.VMEM((3, n_tensor, rows, width), BF16),
            pltpu.VMEM((2, n_tensor, rows, width), BF16),
            pltpu.VMEM((2, 2, n_tensor, rows, width), BF16),
            pltpu.VMEM((rows, width), F32),
            pltpu.VMEM((2, rows, width), BF16),
            pltpu.VMEM((rows, width), BF16),
            pltpu.VMEM((rows, 3 * cols), F32),
            pltpu.VMEM((rows, 128), F32),
            pltpu.VMEM((rows, cols), F32),
            pltpu.VMEM((rows, 3 * cols), BF16),
            pltpu.VMEM((2, n_bits, rows, width), BF16),
            pltpu.VMEM((2, n_bits, rows, width), BF16),
            dma((3, 2, n_tensor)),
            dma((3, n_tensor)),
            dma((2, n_tensor)),
            dma((2, 2, n_tensor)),
            dma((2, n_bits)),
            dma((2, n_bits)),
            dma((2,)),
            dma((2,)),
            dma((8,)),
        ],
        compiler_params=pltpu.CompilerParams(
            collective_id=0, has_side_effects=True, vmem_limit_bytes=48 * 1024 * 1024
        ),
    )(fwd, grad, park, gain, wq, wk, wv, wo, offs, mirror)


def solution(mesh):
    in_specs = (
        P("section", None, "tensor"),
        P("section", None, "tensor"),
        P("section", None, "tensor"),
        P("section", None),
        P("section", None, "tensor"),
        P("section", None, "tensor"),
        P("section", None, "tensor"),
        P("section", "tensor", None),
        P("section", None, None),
        P(),
    )
    out_specs = (P("section", None, "tensor"),) * 3
    step = functools.partial(local_step, mesh.shape["tensor"], mesh.shape["section"])
    return jax.shard_map(step, mesh=mesh, in_specs=in_specs, out_specs=out_specs, check_vma=False)
```

```python
import functools

import jax
import jax.numpy as jnp
from jax import lax
from jax.experimental import pallas as pl
from jax.experimental.pallas import tpu as pltpu
from jax.sharding import PartitionSpec as P

HD = 64
SPAN = 8
MESH = pl.DeviceIdType.MESH
F32 = jnp.float32
BF16 = jnp.bfloat16

NN = (((1,), (0,)), ((), ()))
NT = (((1,), (1,)), ((), ()))
TN = (((0,), (0,)), ((), ()))


def dot(a, b, dims):
    return lax.dot_general(a, b, dims, preferred_element_type=F32)


def within(value, size):
    return jnp.logical_and(value >= 0, value < size)


def kernel(
    n_tensor, n_section, n_bits, blocked,
    fwd_ref, grad_ref, park_ref, gain_ref, wq_ref, wk_ref, wv_ref, wo_hbm, offs_ref, mirror_ref,
    next_ref, prev_ref, pnew_ref,
    w, wo, full, part, arrived, acc, stage, zeros, qkv, ssq, dctx, dqkv, got, cur,
    ag_send, ag_recv, rs_send, rs_recv, swap_send, swap_recv, pass_send, pass_recv, local,
):
    t = lax.axis_index("tensor")
    s = lax.axis_index("section")
    rows, width = fwd_ref.shape[1], fwd_ref.shape[2]
    features = width * n_tensor
    cols = wq_ref.shape[2]
    heads = cols // HD
    blocks = offs_ref.shape[2]

    def mate(bit):
        return s + (1 - 2 * ((s // (1 << bit)) % 2)) * (1 << bit)

    barrier = pltpu.get_barrier_semaphore()

    def greet(ok, where):
        @pl.when(ok)
        def _():
            pl.semaphore_signal(barrier, inc=1, device_id=where, device_id_type=MESH)

    greet(t > 0, {"tensor": t - 1})
    greet(t < n_tensor - 1, {"tensor": t + 1})
    greet(s > 0, {"section": s - 1})
    greet(s < n_section - 1, {"section": s + 1})
    for bit in range(n_bits):
        pl.semaphore_signal(barrier, inc=1, device_id={"section": mate(bit)}, device_id_type=MESH)

    loads = [
        pltpu.make_async_copy(fwd_ref.at[0], full.at[0, t], local.at[0]),
        pltpu.make_async_copy(grad_ref.at[0], full.at[1, t], local.at[1]),
        pltpu.make_async_copy(wq_ref.at[0], w.at[:, pl.ds(0, cols)], local.at[2]),
        pltpu.make_async_copy(wk_ref.at[0], w.at[:, pl.ds(cols, cols)], local.at[3]),
        pltpu.make_async_copy(wv_ref.at[0], w.at[:, pl.ds(2 * cols, cols)], local.at[4]),
        pltpu.make_async_copy(wo_hbm if blocked else wo_hbm.at[0], wo, local.at[5]),
    ]
    for load in loads:
        load.start()

    def one(ok):
        return jnp.where(ok, 1, 0)

    pl.semaphore_wait(
        barrier,
        n_bits + one(t > 0) + one(t < n_tensor - 1) + one(s > 0) + one(s < n_section - 1),
    )

    def ag_copy(a, b, way, src):
        return pltpu.make_async_remote_copy(
            src_ref=src, dst_ref=full.at[a, b],
            send_sem=ag_send.at[a, way, b], recv_sem=ag_recv.at[a, b],
            device_id={"tensor": t + 1 - 2 * way}, device_id_type=MESH,
        )

    def ag_own(a, src):
        for way in range(2):
            @pl.when(within(t + 1 - 2 * way, n_tensor))
            def _():
                ag_copy(a, t, way, src).start()

    def ag_round(a, k, consume):
        def step(way, carry):
            b = t + (1 + k) * (2 * way - 1)

            @pl.when(within(b, n_tensor))
            def _():
                ag_copy(a, b, way, full.at[a, b]).wait_recv()

                @pl.when(within(t + 1 - 2 * way, n_tensor))
                def _():
                    ag_copy(a, b, way, full.at[a, b]).start()

                consume(b)

            return carry

        lax.fori_loop(0, 2, step, 0)

    def swap_copy(a, bit):
        if bit == n_bits - 1:
            src = (park_ref if a == 0 else fwd_ref).at[0]
        else:
            src = got.at[a, bit + 1] if bit == n_bits - 2 else cur.at[a, bit + 1]
        return pltpu.make_async_remote_copy(
            src_ref=src, dst_ref=got.at[a, bit],
            send_sem=swap_send.at[a, bit], recv_sem=swap_recv.at[a, bit],
            device_id={"section": mate(bit)}, device_id_type=MESH,
        )

    def swap_finish(a, bit):
        swap_copy(a, bit).wait_recv()
        if bit < n_bits - 1:
            mine = got[a, bit + 1] if bit == n_bits - 2 else cur[a, bit + 1]
            flag = lax.shift_right_logical(mirror_ref[0], bit) & 1
            chosen = jnp.full((rows, width), flag, jnp.int32) == 1
            cur[a, bit] = jnp.where(chosen, got[a, bit].astype(F32), mine.astype(F32)).astype(BF16)
        if bit > 0:
            swap_copy(a, bit - 1).start()

    swap_copy(0, n_bits - 1).start()
    ag_own(0, fwd_ref.at[0])

    def gain_block(b):
        if blocked:
            return gain_ref[b]
        return gain_ref[0:1, pl.ds(pl.multiple_of(b * width, 128), width)]

    def w_rows(b):
        return w[pl.ds(pl.multiple_of(b * width, 64), width), :]

    def wo_block(b):
        if blocked:
            return wo[b]
        return wo[:, pl.ds(pl.multiple_of(b * width, 128), width)]

    def add_qkv(a, b):
        x = full[a, b].astype(F32)
        ssq[...] += jnp.broadcast_to(jnp.sum(x * x, axis=1, keepdims=True), ssq.shape)
        qkv[...] += dot((x * gain_block(b)).astype(BF16), w_rows(b), NN)

    def add_dctx(b):
        dctx[...] += dot(full[1, b], wo_block(b), NT)

    def clear():
        ssq[...] = jnp.zeros_like(ssq)
        qkv[...] = jnp.zeros_like(qkv)

    clear()
    dctx[...] = jnp.zeros_like(dctx)
    zeros[...] = jnp.zeros_like(zeros)
    for load in loads:
        load.wait()
    add_qkv(0, t)
    add_dctx(t)

    first = [functools.partial(swap_finish, 0, bit) for bit in reversed(range(n_bits))]
    first[0]()

    def round_one(k, carry):
        ag_round(0, k, functools.partial(add_qkv, 0))

        @pl.when(k == 0)
        def _():
            ag_own(1, grad_ref.at[0])

        @pl.when(k == min(1, n_tensor - 2))
        def _():
            for finish in first[1:]:
                finish()
            full[2, t] = cur[0, 0]
            swap_copy(1, n_bits - 1).start()

        return carry

    lax.fori_loop(0, n_tensor - 1, round_one, 0)

    lane = lax.broadcasted_iota(jnp.int32, (rows, cols), 1)

    def masked(value):
        return jnp.concatenate(
            [jnp.where(lane // HD == h, value, 0.0) for h in range(heads)], axis=0
        ).astype(BF16)

    def merged(stacked):
        total = stacked[:rows]
        for h in range(1, heads):
            total = jnp.where(lane // HD == h, stacked[h * rows:(h + 1) * rows], total)
        return total

    def places(which, axis):
        index = lax.broadcasted_iota(jnp.int32, (heads * rows, rows), axis) & (rows - 1)
        block = lax.shift_right_logical(index, 3)
        value = index & (SPAN - 1)
        for b in range(blocks):
            value = value + jnp.where(block == b, offs_ref[0, which, b], 0)
        return value

    def attend(which):
        inverse = lax.rsqrt(ssq[:, 0:1] / features + 1e-05)
        scaled = qkv[...] * inverse
        q = masked(scaled[:, :cols])
        k = scaled[:, cols:2 * cols].astype(BF16)
        v = scaled[:, 2 * cols:].astype(BF16)
        scores = dot(q, k, NT) * (HD ** -0.5)
        scores = jnp.where(places(which, 0) >= places(which, 1), scores, -1e30)
        expd = jnp.exp(scores - jnp.max(scores, axis=1, keepdims=True))
        weights = expd / jnp.sum(expd, axis=1, keepdims=True)
        return inverse, q, k, v, weights

    def rs_copy(a, d, way):
        return pltpu.make_async_remote_copy(
            src_ref=part.at[a, d], dst_ref=arrived.at[a, way, d],
            send_sem=rs_send.at[a, d], recv_sem=rs_recv.at[a, way, d],
            device_id={"tensor": t + 1 - 2 * way}, device_id_type=MESH,
        )

    def rs_begin(a, term):
        def step(i, carry):
            d = jnp.where(t < n_tensor // 2, n_tensor - 1 - i, i)
            part[a, d] = term(d).astype(BF16)
            return carry

        lax.fori_loop(0, n_tensor, step, 0)
        acc[...] = full[a, t].astype(F32) + part[a, t].astype(F32)

    def rs_launch(a, j):
        for way in range(2):
            d = n_tensor - 1 - j if way == 0 else j

            @pl.when(t == way * (n_tensor - 1))
            def _():
                @pl.when(j > 0)
                def _():
                    rs_copy(a, d + 1 - 2 * way, way).wait_send()

                rs_copy(a, d, way).start()

    def rs_tick(a, tick):
        def step(way, carry):
            nth = tick - ((1 - way) * t + way * (n_tensor - 1 - t))
            d = (1 - way) * (n_tensor - 1 - nth) + way * nth
            sign = 1 - 2 * way
            ahead = (d - t) * sign
            expected = jnp.logical_and(nth >= 0, ahead >= 0)

            @pl.when(jnp.logical_and(expected, within(t - sign, n_tensor)))
            def _():
                rs_copy(a, d, way).wait_recv()

                @pl.when(ahead > 0)
                def _():
                    part[a, d] = (part[a, d].astype(F32) + arrived[a, way, d].astype(F32)).astype(BF16)
                    rs_copy(a, d, way).start()

                @pl.when(ahead == 0)
                def _():
                    acc[...] += arrived[a, way, d].astype(F32)

            return carry

        lax.fori_loop(0, 2, step, 0)

    def pass_copy(a):
        return pltpu.make_async_remote_copy(
            src_ref=stage.at[a], dst_ref=(next_ref if a == 0 else prev_ref).at[0],
            send_sem=pass_send.at[a], recv_sem=pass_recv.at[a],
            device_id={"section": s + 1 - 2 * a}, device_id_type=MESH,
        )

    def pass_on(a):
        stage[a] = acc[...].astype(BF16)

        @pl.when(within(s + 1 - 2 * a, n_section))
        def _():
            pass_copy(a).start()

    def zero_copy(a):
        return pltpu.make_async_copy(zeros, (next_ref if a == 0 else prev_ref).at[0], local.at[6])

    @pl.when(s == 0)
    def _():
        zero_copy(0).start()

    @pl.when(s == n_section - 1)
    def _():
        zero_copy(1).start()

    inverse, q, k, v, weights = attend(0)
    context = merged(dot(weights.astype(BF16), v, NN)).astype(BF16)
    rs_begin(0, lambda d: dot(context, wo_block(d), NN))

    def round_two(k, carry):
        rs_launch(0, k)
        ag_round(1, k, add_dctx)

        @pl.when(k == 0)
        def _():
            ag_own(2, full.at[2, t])

        rs_tick(0, k + 1)
        return carry

    lax.fori_loop(0, n_tensor - 1, round_two, 0)
    pass_on(0)
    clear()
    add_qkv(2, t)

    second = [functools.partial(swap_finish, 1, bit) for bit in reversed(range(n_bits))]

    def round_three(k, carry):
        ag_round(2, k, functools.partial(add_qkv, 2))

        @pl.when(k == 0)
        def _():
            for finish in second:
                finish()
            pltpu.make_async_copy(cur.at[1, 0], pnew_ref.at[0], local.at[7]).start()

        return carry

    lax.fori_loop(0, n_tensor - 1, round_three, 0)

    inverse, q, k, v, weights = attend(1)
    dc = masked(dctx[...])
    dweights = dot(dc, v, NT)
    dscores = weights * (dweights - jnp.sum(dweights * weights, axis=1, keepdims=True))
    dscores = (dscores * (HD ** -0.5)).astype(BF16)
    dqkv[:, :cols] = merged(dot(dscores, k, NN)).astype(BF16)
    dqkv[:, cols:2 * cols] = dot(dscores, q, TN).astype(BF16)
    dqkv[:, 2 * cols:] = dot(weights.astype(BF16), dc, TN).astype(BF16)
    pull = dqkv[...]
    along = jnp.sum(pull.astype(F32) * qkv[...], axis=1, keepdims=True)
    along = along * inverse * inverse * inverse / features

    def back_term(d):
        dnormed = dot(pull, w_rows(d), NT)
        return inverse * (dnormed * gain_block(d)) - full[2, d].astype(F32) * along

    rs_begin(1, back_term)

    def round_four(j, carry):
        rs_launch(1, j)
        rs_tick(1, j + 1)
        return carry

    lax.fori_loop(0, n_tensor - 1, round_four, 0)
    pass_on(1)

    def drain(b, carry):
        for way in range(2):
            sent = (b <= t) if way == 0 else (b >= t)

            @pl.when(jnp.logical_and(sent, within(t + 1 - 2 * way, n_tensor)))
            def _():
                for a in range(3):
                    ag_copy(a, b, way, full.at[a, b]).wait_send()

        last = jnp.where(t == 0, 1, jnp.where(t == n_tensor - 1, n_tensor - 2, b))

        @pl.when(jnp.logical_and(b != t, b == last))
        def _():
            for a in range(2):
                rs_copy(a, b, 0).wait_send()

        return carry

    lax.fori_loop(0, n_tensor, drain, 0)
    for a in range(2):
        for bit in range(n_bits):
            swap_copy(a, bit).wait_send()
    pltpu.make_async_copy(cur.at[1, 0], pnew_ref.at[0], local.at[7]).wait()
    for a in range(2):
        edge = 0 if a == 0 else n_section - 1

        @pl.when(s == edge)
        def _():
            zero_copy(a).wait()

        @pl.when(s != edge)
        def _():
            pass_copy(a).wait_recv()

        @pl.when(within(s + 1 - 2 * a, n_section))
        def _():
            pass_copy(a).wait_send()


def hand_over(*refs):
    for i in range(3):
        refs[3 + i][...] = refs[i][...]


def local_step(n_tensor, n_section, fwd, grad, park, gain, wq, wk, wv, wo, offs, mirror):
    _, rows, width = fwd.shape
    features = gain.shape[1]
    cols = wq.shape[2]
    n_bits = n_section.bit_length() - 1
    blocked = width % 128 != 0
    if blocked:
        gain = gain.reshape(n_tensor, 1, width)
        wo = wo[0].reshape(cols, n_tensor, width).transpose(1, 0, 2)
    heads = cols // HD
    any_spec = pl.BlockSpec(memory_space=pl.ANY)
    vmem = pl.BlockSpec(memory_space=pltpu.VMEM)
    smem = pl.BlockSpec(memory_space=pltpu.SMEM)
    out = jax.ShapeDtypeStruct(fwd.shape, BF16)
    dma = pltpu.SemaphoreType.DMA
    results = pl.pallas_call(
        functools.partial(kernel, n_tensor, n_section, n_bits, blocked),
        out_shape=(out, out, out),
        in_specs=[any_spec] * 3 + [vmem] + [any_spec] * 4 + [smem] * 2,
        out_specs=(any_spec,) * 3,
        scratch_shapes=[
            pltpu.VMEM((features, 3 * cols), BF16),
            pltpu.VMEM((n_tensor, cols, width) if blocked else (cols, features), BF16),
            pltpu.VMEM((3, n_tensor, rows, width), BF16),
            pltpu.VMEM((2, n_tensor, rows, width), BF16),
            pltpu.VMEM((2, 2, n_tensor, rows, width), BF16),
            pltpu.VMEM((rows, width), F32),
            pltpu.VMEM((2, rows, width), BF16),
            pltpu.VMEM((rows, width), BF16),
            pltpu.VMEM((rows, 3 * cols), F32),
            pltpu.VMEM((rows, 128), F32),
            pltpu.VMEM((rows, cols), F32),
            pltpu.VMEM((rows, 3 * cols), BF16),
            pltpu.VMEM((2, n_bits, rows, width), BF16),
            pltpu.VMEM((2, n_bits, rows, width), BF16),
            dma((3, 2, n_tensor)),
            dma((3, n_tensor)),
            dma((2, n_tensor)),
            dma((2, 2, n_tensor)),
            dma((2, n_bits)),
            dma((2, n_bits)),
            dma((2,)),
            dma((2,)),
            dma((8,)),
        ],
        compiler_params=pltpu.CompilerParams(
            collective_id=0, has_side_effects=True, vmem_limit_bytes=62 * 1024 * 1024
        ),
    )(fwd, grad, park, gain, wq, wk, wv, wo, offs, mirror)
    return pl.pallas_call(
        hand_over,
        out_shape=(out, out, out),
        in_specs=[vmem] * 3,
        out_specs=(vmem,) * 3,
    )(*results)


def solution(mesh):
    in_specs = (
        P("section", None, "tensor"),
        P("section", None, "tensor"),
        P("section", None, "tensor"),
        P("section", None),
        P("section", None, "tensor"),
        P("section", None, "tensor"),
        P("section", None, "tensor"),
        P("section", "tensor", None),
        P("section", None, None),
        P(),
    )
    out_specs = (P("section", None, "tensor"),) * 3
    step = functools.partial(local_step, mesh.shape["tensor"], mesh.shape["section"])
    return jax.shard_map(step, mesh=mesh, in_specs=in_specs, out_specs=out_specs, check_vma=False)
```

```python
import functools

import jax
import jax.numpy as jnp
from jax import lax
from jax.experimental import pallas as pl
from jax.experimental.pallas import tpu as pltpu
from jax.sharding import PartitionSpec as P

HD = 64
SPAN = 8
MESH = pl.DeviceIdType.MESH
F32 = jnp.float32
BF16 = jnp.bfloat16

NN = (((1,), (0,)), ((), ()))
NT = (((1,), (1,)), ((), ()))
TN = (((0,), (0,)), ((), ()))


def dot(a, b, dims):
    return lax.dot_general(a, b, dims, preferred_element_type=F32)


def within(value, size):
    return jnp.logical_and(value >= 0, value < size)


def kernel(
    n_tensor, n_section, n_bits, blocked,
    fwd_ref, grad_ref, park_ref, gain_ref, wq_ref, wk_ref, wv_ref, wo_hbm, offs_ref, mirror_ref,
    next_ref, prev_ref, pnew_ref,
    w, wo, full, part, arrived, acc, stage, zeros, qkv, ssq, dctx, dqkv, got, cur,
    ag_send, ag_recv, rs_send, rs_recv, swap_send, swap_recv, pass_send, pass_recv, local,
):
    t = lax.axis_index("tensor")
    s = lax.axis_index("section")
    rows, width = fwd_ref.shape[1], fwd_ref.shape[2]
    features = width * n_tensor
    cols = wq_ref.shape[2]
    heads = cols // HD
    blocks = offs_ref.shape[2]

    def mate(bit):
        return s + (1 - 2 * ((s // (1 << bit)) % 2)) * (1 << bit)

    barrier = pltpu.get_barrier_semaphore()

    def greet(ok, where):
        @pl.when(ok)
        def _():
            pl.semaphore_signal(barrier, inc=1, device_id=where, device_id_type=MESH)

    greet(t > 0, {"tensor": t - 1})
    greet(t < n_tensor - 1, {"tensor": t + 1})
    greet(s > 0, {"section": s - 1})
    greet(s < n_section - 1, {"section": s + 1})
    for bit in range(n_bits):
        pl.semaphore_signal(barrier, inc=1, device_id={"section": mate(bit)}, device_id_type=MESH)

    loads = [
        pltpu.make_async_copy(fwd_ref.at[0], full.at[0, t], local.at[0]),
        pltpu.make_async_copy(grad_ref.at[0], full.at[1, t], local.at[1]),
        pltpu.make_async_copy(wq_ref.at[0], w.at[:, pl.ds(0, cols)], local.at[2]),
        pltpu.make_async_copy(wk_ref.at[0], w.at[:, pl.ds(cols, cols)], local.at[3]),
        pltpu.make_async_copy(wv_ref.at[0], w.at[:, pl.ds(2 * cols, cols)], local.at[4]),
        pltpu.make_async_copy(wo_hbm if blocked else wo_hbm.at[0], wo, local.at[5]),
    ]
    for load in loads:
        load.start()

    def one(ok):
        return jnp.where(ok, 1, 0)

    pl.semaphore_wait(
        barrier,
        n_bits + one(t > 0) + one(t < n_tensor - 1) + one(s > 0) + one(s < n_section - 1),
    )

    def ag_copy(a, b, way, src):
        return pltpu.make_async_remote_copy(
            src_ref=src, dst_ref=full.at[a, b],
            send_sem=ag_send.at[a, way, b], recv_sem=ag_recv.at[a, b],
            device_id={"tensor": t + 1 - 2 * way}, device_id_type=MESH,
        )

    def ag_own(a, src):
        for way in range(2):
            @pl.when(within(t + 1 - 2 * way, n_tensor))
            def _():
                ag_copy(a, t, way, src).start()

    def ag_round(a, k, consume):
        def step(way, carry):
            b = t + (1 + k) * (2 * way - 1)

            @pl.when(within(b, n_tensor))
            def _():
                ag_copy(a, b, way, full.at[a, b]).wait_recv()

                @pl.when(within(t + 1 - 2 * way, n_tensor))
                def _():
                    ag_copy(a, b, way, full.at[a, b]).start()

                consume(b)

            return carry

        lax.fori_loop(0, 2, step, 0)

    def swap_copy(a, bit):
        if bit == n_bits - 1:
            src = (park_ref if a == 0 else fwd_ref).at[0]
        else:
            src = got.at[a, bit + 1] if bit == n_bits - 2 else cur.at[a, bit + 1]
        return pltpu.make_async_remote_copy(
            src_ref=src, dst_ref=got.at[a, bit],
            send_sem=swap_send.at[a, bit], recv_sem=swap_recv.at[a, bit],
            device_id={"section": mate(bit)}, device_id_type=MESH,
        )

    def swap_finish(a, bit):
        swap_copy(a, bit).wait_recv()
        if bit < n_bits - 1:
            mine = got[a, bit + 1] if bit == n_bits - 2 else cur[a, bit + 1]
            flag = lax.shift_right_logical(mirror_ref[0], bit) & 1
            chosen = jnp.full((rows, width), flag, jnp.int32) == 1
            cur[a, bit] = jnp.where(chosen, got[a, bit].astype(F32), mine.astype(F32)).astype(BF16)
        if bit > 0:
            swap_copy(a, bit - 1).start()

    swap_copy(0, n_bits - 1).start()
    ag_own(0, fwd_ref.at[0])
    ag_own(1, grad_ref.at[0])

    def gain_block(b):
        if blocked:
            return gain_ref[b]
        return gain_ref[0:1, pl.ds(pl.multiple_of(b * width, 128), width)]

    def w_rows(b):
        return w[pl.ds(pl.multiple_of(b * width, 64), width), :]

    def wo_block(b):
        if blocked:
            return wo[b]
        return wo[:, pl.ds(pl.multiple_of(b * width, 128), width)]

    def add_qkv(a, b):
        x = full[a, b].astype(F32)
        ssq[...] += jnp.broadcast_to(jnp.sum(x * x, axis=1, keepdims=True), ssq.shape)
        qkv[...] += dot((x * gain_block(b)).astype(BF16), w_rows(b), NN)

    def add_dctx(b):
        dctx[...] += dot(full[1, b], wo_block(b), NT)

    def clear():
        ssq[...] = jnp.zeros_like(ssq)
        qkv[...] = jnp.zeros_like(qkv)

    clear()
    dctx[...] = jnp.zeros_like(dctx)
    zeros[...] = jnp.zeros_like(zeros)
    for load in loads:
        load.wait()
    add_qkv(0, t)
    add_dctx(t)

    first = [functools.partial(swap_finish, 0, bit) for bit in reversed(range(n_bits))]
    first[0]()

    def round_one(k, carry):
        ag_round(0, k, functools.partial(add_qkv, 0))
        ag_round(1, k, add_dctx)

        for at in range(n_bits - 1):
            @pl.when(k == min(at, n_tensor - 2))
            def _():
                first[at + 1]()
                if at == n_bits - 2:
                    full[2, t] = cur[0, 0]
                    ag_own(2, full.at[2, t])
                    swap_copy(1, n_bits - 1).start()

        return carry

    lax.fori_loop(0, n_tensor - 1, round_one, 0)

    lane = lax.broadcasted_iota(jnp.int32, (rows, cols), 1)

    def masked(value):
        return jnp.concatenate(
            [jnp.where(lane // HD == h, value, 0.0) for h in range(heads)], axis=0
        ).astype(BF16)

    def merged(stacked):
        total = stacked[:rows]
        for h in range(1, heads):
            total = jnp.where(lane // HD == h, stacked[h * rows:(h + 1) * rows], total)
        return total

    def places(which, axis):
        index = lax.broadcasted_iota(jnp.int32, (heads * rows, rows), axis) & (rows - 1)
        block = lax.shift_right_logical(index, 3)
        value = index & (SPAN - 1)
        for b in range(blocks):
            value = value + jnp.where(block == b, offs_ref[0, which, b], 0)
        return value

    def attend(which):
        inverse = lax.rsqrt(ssq[:, 0:1] / features + 1e-05)
        scaled = qkv[...] * inverse
        q = masked(scaled[:, :cols])
        k = scaled[:, cols:2 * cols].astype(BF16)
        v = scaled[:, 2 * cols:].astype(BF16)
        scores = dot(q, k, NT) * (HD ** -0.5)
        scores = jnp.where(places(which, 0) >= places(which, 1), scores, -1e30)
        expd = jnp.exp(scores - jnp.max(scores, axis=1, keepdims=True))
        weights = expd / jnp.sum(expd, axis=1, keepdims=True)
        return inverse, q, k, v, weights

    def rs_copy(a, d, way):
        return pltpu.make_async_remote_copy(
            src_ref=part.at[a, d], dst_ref=arrived.at[a, way, d],
            send_sem=rs_send.at[a, d], recv_sem=rs_recv.at[a, way, d],
            device_id={"tensor": t + 1 - 2 * way}, device_id_type=MESH,
        )

    def rs_launch(a, j):
        for way in range(2):
            d = n_tensor - 1 - j if way == 0 else j

            @pl.when(t == way * (n_tensor - 1))
            def _():
                if not isinstance(j, int):
                    rs_copy(a, d + 1 - 2 * way, way).wait_send()

                rs_copy(a, d, way).start()

    def rs_begin(a, term):
        def step(i, carry):
            d = jnp.where(t < n_tensor // 2, n_tensor - 1 - i, i)
            part[a, d] = term(d).astype(BF16)

            @pl.when(i == 0)
            def _():
                rs_launch(a, 0)

            return carry

        lax.fori_loop(0, n_tensor, step, 0)
        acc[...] = full[a, t].astype(F32) + part[a, t].astype(F32)

    def rs_tick(a, tick):
        def step(way, carry):
            nth = tick - ((1 - way) * t + way * (n_tensor - 1 - t))
            d = (1 - way) * (n_tensor - 1 - nth) + way * nth
            sign = 1 - 2 * way
            ahead = (d - t) * sign
            expected = jnp.logical_and(nth >= 0, ahead >= 0)

            @pl.when(jnp.logical_and(expected, within(t - sign, n_tensor)))
            def _():
                rs_copy(a, d, way).wait_recv()

                @pl.when(ahead > 0)
                def _():
                    part[a, d] = (part[a, d].astype(F32) + arrived[a, way, d].astype(F32)).astype(BF16)
                    rs_copy(a, d, way).start()

                @pl.when(ahead == 0)
                def _():
                    acc[...] += arrived[a, way, d].astype(F32)

            return carry

        lax.fori_loop(0, 2, step, 0)

    def pass_copy(a):
        return pltpu.make_async_remote_copy(
            src_ref=stage.at[a], dst_ref=(next_ref if a == 0 else prev_ref).at[0],
            send_sem=pass_send.at[a], recv_sem=pass_recv.at[a],
            device_id={"section": s + 1 - 2 * a}, device_id_type=MESH,
        )

    def pass_on(a):
        stage[a] = acc[...].astype(BF16)

        @pl.when(within(s + 1 - 2 * a, n_section))
        def _():
            pass_copy(a).start()

    def zero_copy(a):
        return pltpu.make_async_copy(zeros, (next_ref if a == 0 else prev_ref).at[0], local.at[6])

    @pl.when(s == 0)
    def _():
        zero_copy(0).start()

    @pl.when(s == n_section - 1)
    def _():
        zero_copy(1).start()

    inverse, q, k, v, weights = attend(0)
    context = merged(dot(weights.astype(BF16), v, NN)).astype(BF16)
    rs_begin(0, lambda d: dot(context, wo_block(d), NN))

    clear()
    add_qkv(2, t)

    second = [functools.partial(swap_finish, 1, bit) for bit in reversed(range(n_bits))]

    def round_three(k, carry):
        @pl.when(k > 0)
        def _():
            rs_launch(0, k)

        ag_round(2, k, functools.partial(add_qkv, 2))
        rs_tick(0, k + 1)

        for at in range(n_bits):
            @pl.when(k == min(at, n_tensor - 2))
            def _():
                second[at]()
                if at == n_bits - 1:
                    pltpu.make_async_copy(cur.at[1, 0], pnew_ref.at[0], local.at[7]).start()

        return carry

    lax.fori_loop(0, n_tensor - 1, round_three, 0)
    pass_on(0)

    inverse, q, k, v, weights = attend(1)
    dc = masked(dctx[...])
    dweights = dot(dc, v, NT)
    dscores = weights * (dweights - jnp.sum(dweights * weights, axis=1, keepdims=True))
    dscores = (dscores * (HD ** -0.5)).astype(BF16)
    dqkv[:, :cols] = merged(dot(dscores, k, NN)).astype(BF16)
    dqkv[:, cols:2 * cols] = dot(dscores, q, TN).astype(BF16)
    dqkv[:, 2 * cols:] = dot(weights.astype(BF16), dc, TN).astype(BF16)
    pull = dqkv[...]
    along = jnp.sum(pull.astype(F32) * qkv[...], axis=1, keepdims=True)
    along = along * inverse * inverse * inverse / features

    def back_term(d):
        dnormed = dot(pull, w_rows(d), NT)
        return inverse * (dnormed * gain_block(d)) - full[2, d].astype(F32) * along

    rs_begin(1, back_term)

    def round_four(j, carry):
        @pl.when(j > 0)
        def _():
            rs_launch(1, j)

        rs_tick(1, j + 1)
        return carry

    lax.fori_loop(0, n_tensor - 1, round_four, 0)
    pass_on(1)

    def drain(b, carry):
        for way in range(2):
            sent = (b <= t) if way == 0 else (b >= t)

            @pl.when(jnp.logical_and(sent, within(t + 1 - 2 * way, n_tensor)))
            def _():
                for a in range(3):
                    ag_copy(a, b, way, full.at[a, b]).wait_send()

        last = jnp.where(t == 0, 1, jnp.where(t == n_tensor - 1, n_tensor - 2, b))

        @pl.when(jnp.logical_and(b != t, b == last))
        def _():
            for a in range(2):
                rs_copy(a, b, 0).wait_send()

        return carry

    lax.fori_loop(0, n_tensor, drain, 0)
    for a in range(2):
        for bit in range(n_bits):
            swap_copy(a, bit).wait_send()
    pltpu.make_async_copy(cur.at[1, 0], pnew_ref.at[0], local.at[7]).wait()
    for a in range(2):
        edge = 0 if a == 0 else n_section - 1

        @pl.when(s == edge)
        def _():
            zero_copy(a).wait()

        @pl.when(s != edge)
        def _():
            pass_copy(a).wait_recv()

        @pl.when(within(s + 1 - 2 * a, n_section))
        def _():
            pass_copy(a).wait_send()


def hand_over(*refs):
    for i in range(3):
        refs[3 + i][...] = refs[i][...]


def local_step(n_tensor, n_section, fwd, grad, park, gain, wq, wk, wv, wo, offs, mirror):
    _, rows, width = fwd.shape
    features = gain.shape[1]
    cols = wq.shape[2]
    n_bits = n_section.bit_length() - 1
    blocked = width % 128 != 0
    if blocked:
        gain = gain.reshape(n_tensor, 1, width)
        wo = wo[0].reshape(cols, n_tensor, width).transpose(1, 0, 2)
    heads = cols // HD
    any_spec = pl.BlockSpec(memory_space=pl.ANY)
    vmem = pl.BlockSpec(memory_space=pltpu.VMEM)
    smem = pl.BlockSpec(memory_space=pltpu.SMEM)
    out = jax.ShapeDtypeStruct(fwd.shape, BF16)
    dma = pltpu.SemaphoreType.DMA
    results = pl.pallas_call(
        functools.partial(kernel, n_tensor, n_section, n_bits, blocked),
        out_shape=(out, out, out),
        in_specs=[any_spec] * 3 + [vmem] + [any_spec] * 4 + [smem] * 2,
        out_specs=(any_spec,) * 3,
        scratch_shapes=[
            pltpu.VMEM((features, 3 * cols), BF16),
            pltpu.VMEM((n_tensor, cols, width) if blocked else (cols, features), BF16),
            pltpu.VMEM((3, n_tensor, rows, width), BF16),
            pltpu.VMEM((2, n_tensor, rows, width), BF16),
            pltpu.VMEM((2, 2, n_tensor, rows, width), BF16),
            pltpu.VMEM((rows, width), F32),
            pltpu.VMEM((2, rows, width), BF16),
            pltpu.VMEM((rows, width), BF16),
            pltpu.VMEM((rows, 3 * cols), F32),
            pltpu.VMEM((rows, 128), F32),
            pltpu.VMEM((rows, cols), F32),
            pltpu.VMEM((rows, 3 * cols), BF16),
            pltpu.VMEM((2, n_bits, rows, width), BF16),
            pltpu.VMEM((2, n_bits, rows, width), BF16),
            dma((3, 2, n_tensor)),
            dma((3, n_tensor)),
            dma((2, n_tensor)),
            dma((2, 2, n_tensor)),
            dma((2, n_bits)),
            dma((2, n_bits)),
            dma((2,)),
            dma((2,)),
            dma((8,)),
        ],
        compiler_params=pltpu.CompilerParams(
            collective_id=0, has_side_effects=True, vmem_limit_bytes=62 * 1024 * 1024
        ),
    )(fwd, grad, park, gain, wq, wk, wv, wo, offs, mirror)
    return pl.pallas_call(
        hand_over,
        out_shape=(out, out, out),
        in_specs=[vmem] * 3,
        out_specs=(vmem,) * 3,
    )(*results)


def solution(mesh):
    in_specs = (
        P("section", None, "tensor"),
        P("section", None, "tensor"),
        P("section", None, "tensor"),
        P("section", None),
        P("section", None, "tensor"),
        P("section", None, "tensor"),
        P("section", None, "tensor"),
        P("section", "tensor", None),
        P("section", None, None),
        P(),
    )
    out_specs = (P("section", None, "tensor"),) * 3
    step = functools.partial(local_step, mesh.shape["tensor"], mesh.shape["section"])
    return jax.shard_map(step, mesh=mesh, in_specs=in_specs, out_specs=out_specs, check_vma=False)
```
